256 devices in a mesh: seq: 128 (over z, x, y), hid: 2 (over core).
Axes of the slice: x: 4, y: 4, z: 8, core: 2. Of those that a mesh axis runs over, the one named last changes fastest.
Arguments:
- tokens: bfloat16 [16384, 768], P('seq', 'hid'), may hold values from -6 to 6
- norm_gain: float32 [768], P('hid'), may hold values from 0.5 to 2
- in_weight: bfloat16 [3, 768, 768], P(None, None, 'hid'), may hold values from -0.21875 to 0.21875
- short_filter: float32 [3, 3, 768], P(None, None, 'hid'), may hold values from -1 to 1
- spectrum: float32 [2, 16384, 768], P(None, 'seq', 'hid'), may hold values from -6 to 6
- out_weight: bfloat16 [768, 768], P('hid'), may hold values from -0.21875 to 0.21875
- mlp_gain: float32 [768], P('hid'), may hold values from 0.4 to 2.3
- up_weight: bfloat16 [768, 3072], P(None, 'hid'), may hold values from -0.21650635 to 0.21650635
- down_weight: bfloat16 [768, 3072], P(None, 'hid'), may hold values from -0.15155445 to 0.15155445
- cotangent: bfloat16 [16384, 768], P('seq', 'hid'), may hold values from -6 to 6
Outputs:
- output: bfloat16 [16384, 768], P('seq', 'hid')
- grad_tokens: bfloat16 [16384, 768], P('seq', 'hid')
- grad_up: float32 [768, 3072], P('seq', 'hid')
- grad_down: float32 [768, 3072], P('seq', 'hid')
The draws below stay inside these ranges and needn't reach their ends.
All inputs are finite; a program needn't handle non-finite values.
Results may differ from the reference program's by a relative error of at most 0.0095.
Values may be sent and summed in bfloat16 or wider, within the bound.
A program may use at most 128 MiB of HBM per device.

```python
import math
import jax
import jax.numpy as jnp
from jax import lax

D = 768
FF = 3072
TOK_DEV = 128
TAPS = 3
SPLIT = 128
TOKENS = 16384


def spiked_field(key):
    base = jax.random.normal(jax.random.fold_in(key, 11), (TOKENS, D), jnp.float32)
    pairing = jax.random.permutation(jax.random.fold_in(key, 12), SPLIT)
    row_block = jnp.arange(TOKENS) // TOK_DEV
    col_block = jnp.arange(D) // (D // SPLIT)
    marked = pairing[row_block][:, None] == col_block[None, :]
    return base * jnp.where(marked, 3.0, 1.0)


def shared_matrix(key):
    return jnp.clip(jax.random.normal(jax.random.fold_in(key, 21), (D, FF), jnp.float32), -6.0, 6.0)


def draw_tokens(key, part):
    field = spiked_field(key)
    return jnp.clip(field, -6.0, 6.0).astype(jnp.bfloat16)


def draw_cotangent(key, part):
    field = spiked_field(key)
    key = jax.random.fold_in(key, 2)
    own = jax.random.normal(key, (TOKENS, D), jnp.float32)
    return jnp.clip(0.8 * field + 0.6 * own, -6.0, 6.0).astype(jnp.bfloat16)


def draw_up_weight(key, part):
    common = shared_matrix(key)
    return (common / jnp.sqrt(jnp.float32(D))).astype(jnp.bfloat16)


def draw_down_weight(key, part):
    common = shared_matrix(key)
    key = jax.random.fold_in(key, 3)
    own = jnp.clip(jax.random.normal(key, (D, FF), jnp.float32), -6.0, 6.0)
    return ((0.8 * common + 0.6 * own) / jnp.sqrt(jnp.float32(FF))).astype(jnp.bfloat16)


def draw_mlp_gain(key, part):
    key = jax.random.fold_in(key, 4)
    place = jnp.arange(D, dtype=jnp.float32) / (D - 1)
    trend = 0.6 * 3.0 ** place
    rough = jnp.exp(jax.random.uniform(key, (D,), jnp.float32, -0.22, 0.22))
    return trend * rough


def block_levels(stream_key, extent, pieces, least, largest):
    factor_of, own = 1.0, jax.random.fold_in(stream_key, 6)
    for axis_at, parts in pieces:
        draws = jnp.exp(jax.random.uniform(jax.random.fold_in(own, axis_at), (parts,), jnp.float32, least / len(pieces), largest / len(pieces)))
        factor_of = factor_of * jnp.repeat(draws, extent[axis_at] // parts).reshape([-1 if axis == axis_at else 1 for axis in range(len(extent))])
    return factor_of


def normal_values(own_key, shape, scale, most, cuts=(), held_as=jnp.bfloat16):
    drawn = scale * jax.random.normal(own_key, shape, jnp.float32)
    if cuts:
        drawn = drawn * block_levels(own_key, shape, cuts, -0.22, 0.18)
    return jnp.clip(drawn, -most, most).astype(held_as)


def setup_inputs(seed: int = 0) -> dict:
    key_of = jax.random.split(jax.random.key(seed), 11)
    tokens = draw_tokens(jax.random.fold_in(key_of[10], 71), 0)
    norm_gain = jnp.clip(jnp.exp(math.log(2.0) - 1.3862944 * jax.random.uniform(key_of[1], (D,), jnp.float32) ** block_levels(key_of[1], (D,), ((0, 2),), -0.2, 0.2)), 0.5, 2.0)
    in_weight = normal_values(key_of[2], (3, D, D), D ** -0.5, 0.21875, ((2, 2),))
    short_filter = jnp.clip(jax.random.uniform(key_of[3], (3, TAPS, D), jnp.float32, -1.0, 1.0) * block_levels(key_of[3], (3, TAPS, D), ((2, 2),), -0.4, 0.0), -1.0, 1.0)
    spectrum = normal_values(key_of[4], (2, TOKENS, D), 1.0, 6.0, ((1, 128), (2, 2)), jnp.float32)
    out_weight = normal_values(key_of[5], (D, D), D ** -0.5, 0.21875, ((0, 2),))
    mlp_gain = draw_mlp_gain(jax.random.fold_in(key_of[10], 71), 0)
    up_weight = draw_up_weight(jax.random.fold_in(key_of[10], 71), 0)
    down_weight = draw_down_weight(jax.random.fold_in(key_of[10], 71), 0)
    cotangent = draw_cotangent(jax.random.fold_in(key_of[10], 71), 0)
    return {"tokens": tokens, "norm_gain": norm_gain, "in_weight": in_weight, "short_filter": short_filter, "spectrum": spectrum, "out_weight": out_weight, "mlp_gain": mlp_gain, "up_weight": up_weight, "down_weight": down_weight, "cotangent": cotangent}


EPSILON = 1e-05
GELU_SCALE = 0.7978845608028654

def gelu_value(values):
    inner = GELU_SCALE * (values + 0.044715 * values * values * values)
    return 0.5 * values * (1.0 + jnp.tanh(inner))

def gelu_slope(values):
    tanh_val = jnp.tanh(GELU_SCALE * (values + 0.044715 * values * values * values))
    return 0.5 * (1.0 + tanh_val) + 0.5 * values * (1.0 - tanh_val * tanh_val) * GELU_SCALE * (1.0 + 3.0 * 0.044715 * values * values)

def reversed_bits(position, bit_count):
    result = jnp.zeros_like(position)
    for place in range(bit_count):
        result = result + (position >> place & 1) * (1 << bit_count - 1 - place)
    return result

def natural_kernel(spectrum):
    bit_count = SPLIT.bit_length() - 1
    order = reversed_bits(jnp.arange(SPLIT, dtype=jnp.int32), bit_count).astype(jnp.int32)
    grid = spectrum.reshape(2, SPLIT, TOK_DEV, D)[:, order]
    grid = jnp.transpose(grid, (0, 2, 1, 3)).reshape(2, TOKENS, D)
    return lax.complex(grid[0], grid[1])

def long_conv(signal, kernel):
    return jnp.real(jnp.fft.ifft(jnp.fft.fft(signal, axis=0) * kernel, axis=0))

def reference(tokens, norm_gain, in_weight, short_filter, spectrum, out_weight, mlp_gain, up_weight, down_weight, cotangent):
    tap_count = short_filter.shape[1]
    tokens_f = tokens.astype(jnp.float32)
    scale_in = lax.rsqrt(lax.optimization_barrier(jnp.sum(tokens_f * tokens_f, axis=1)) / D + EPSILON)
    normed_in = tokens_f * scale_in[:, None]
    inputs_b = (normed_in * norm_gain[None, :]).astype(jnp.bfloat16)
    projected = jnp.stack([jnp.dot(inputs_b, in_weight[proj_index], preferred_element_type=jnp.float32) for proj_index in range(3)])
    padded = jnp.pad(projected, ((0, 0), (tap_count - 1, 0), (0, 0)))
    shorted = jnp.zeros_like(projected)
    for tap_index in range(tap_count):
        begin = tap_count - 1 - tap_index
        shorted = shorted + short_filter[:, tap_index, None, :] * padded[:, begin:begin + TOKENS, :]
    signal = shorted[1] * shorted[0]
    kernel = natural_kernel(spectrum)
    conv = long_conv(signal, kernel)
    mixed_y = (shorted[2] * conv).astype(jnp.bfloat16)
    resid_one = tokens_f + jnp.dot(mixed_y, out_weight, preferred_element_type=jnp.float32)
    scale_two = lax.rsqrt(lax.optimization_barrier(jnp.sum(resid_one * resid_one, axis=1)) / D + EPSILON)
    normed_two = resid_one * scale_two[:, None]
    mlp_in = (normed_two * mlp_gain[None, :]).astype(jnp.bfloat16)
    pre = jnp.dot(mlp_in, up_weight, preferred_element_type=jnp.float32)
    hidden = gelu_value(pre).astype(jnp.bfloat16)
    down_terms = jnp.dot(hidden, down_weight.T, preferred_element_type=jnp.float32)
    output = (resid_one + down_terms).astype(jnp.bfloat16)
    cot_f = cotangent.astype(jnp.float32)
    d_hidden = jnp.dot(cotangent, down_weight, preferred_element_type=jnp.float32)
    d_pre = (d_hidden * gelu_slope(pre)).astype(jnp.bfloat16)
    grad_scale = 1.0 / math.sqrt(TOKENS)
    grad_up = jnp.dot(mlp_in.T, d_pre, preferred_element_type=jnp.float32) * grad_scale
    grad_down = jnp.dot(cotangent.T, hidden, preferred_element_type=jnp.float32) * grad_scale
    d_mlp_in = jnp.dot(d_pre, up_weight.T, preferred_element_type=jnp.float32)
    d_n2 = d_mlp_in * mlp_gain[None, :]
    inner_two = lax.optimization_barrier(jnp.sum(d_n2 * normed_two, axis=1)) / D
    d_resid = cot_f + scale_two[:, None] * (d_n2 - normed_two * inner_two[:, None])
    d_resid_b = d_resid.astype(jnp.bfloat16)
    d_mixed = jnp.dot(d_resid_b, out_weight.T, preferred_element_type=jnp.float32)
    d_conv = d_mixed * shorted[2]
    d_outer = d_mixed * conv
    d_signal = long_conv(d_conv, jnp.conj(kernel))
    d_short = jnp.stack([d_signal * shorted[1], d_signal * shorted[0], d_outer])
    padded_back = jnp.pad(d_short, ((0, 0), (0, tap_count - 1), (0, 0)))
    d_proj = jnp.zeros_like(d_short)
    for tap_index in range(tap_count):
        d_proj = d_proj + short_filter[:, tap_index, None, :] * padded_back[:, tap_index:tap_index + TOKENS, :]
    d_proj = d_proj.astype(jnp.bfloat16)
    d_inputs = jnp.zeros((TOKENS, D), jnp.float32)
    for proj_index in range(3):
        d_inputs = d_inputs + jnp.dot(d_proj[proj_index], in_weight[proj_index].T, preferred_element_type=jnp.float32)
    d_n1 = d_inputs * norm_gain[None, :]
    inner_one = lax.optimization_barrier(jnp.sum(d_n1 * normed_in, axis=1)) / D
    grad_tokens = (d_resid + scale_in[:, None] * (d_n1 - normed_in * inner_one[:, None])).astype(jnp.bfloat16)
    return (output, grad_tokens, grad_up, grad_down)
```

```python
import math

import jax
import jax.numpy as jnp
import ml_dtypes
import numpy as np
from jax import lax
from jax.experimental import pallas as pl
from jax.experimental.pallas import tpu as pltpu
from jax.sharding import PartitionSpec as P

EPSILON = 1e-05
GELU_SCALE = 0.7978845608028654
MESH = pl.DeviceIdType.MESH
F32 = jnp.float32
BF16 = jnp.bfloat16
GRIDS = {128: (8, 4, 4), 8: (2, 2, 2), 16: (2, 4, 2)}
TOK = 128
HALO = 16


def up_to(value, unit):
    return -(-value // unit) * unit


class Names:
    def __getattr__(self, key):
        return key


class Box(dict):
    __getattr__ = dict.__getitem__


S = Names()


class Plan:
    def __init__(self, count, width, units):
        self.n = count
        self.Z, self.X, self.Y = GRIDS[count]
        self.P = self.X * self.Y
        self.D = width
        self.C = width // 2
        self.F = units
        self.KC = self.C // count
        self.KP = self.KC
        while (self.Z * self.KP) % 16:
            self.KP += 1
        self.R = count * self.KP
        self.ZB = self.C // self.Z
        self.PB = self.Z * self.KP
        self.E = width // count
        self.EP = up_to(self.E, 8)
        self.Q3 = up_to(2 * self.Z * self.E, 128)


def tables(plan):
    n, Z, X, Y, PP = plan.n, plan.Z, plan.X, plan.Y, plan.P
    KC, KP, R = plan.KC, plan.KP, plan.R
    bits = n.bit_length() - 1
    rev = np.array([int(format(q, f"0{bits}b")[::-1], 2) for q in range(n)])
    rows = np.arange(R)
    slot = rows % KP
    source = (rows // KP) % Z * PP + rows // (KP * Z)
    freq = rev[source]
    same = (slot[:, None] == slot[None, :]) & (slot[:, None] < KC)
    angle = 2 * np.pi * ((freq[:, None] * source[None, :]) % n) / n
    first = np.concatenate([same * np.cos(angle), -(same * np.sin(angle))], axis=0)
    u = np.arange(TOK)
    twist = 2 * np.pi * ((freq[:, None] * u[None, :]) % (n * TOK)) / (n * TOK)
    table = 2 * np.pi * ((u[:, None] * u[None, :]) % TOK) / TOK
    inner = np.block([[np.cos(table), -np.sin(table)], [np.sin(table), np.cos(table)]])
    spread = np.zeros((R, plan.C))
    for p in range(PP):
        for z in range(Z):
            for i in range(KC):
                spread[(p * Z + z) * KP + i, z * plan.ZB + p * KC + i] = 1
    feat = np.arange(plan.D)
    e = feat % plan.E
    dest = feat // plan.E
    dz, dx, dy = dest // PP, dest % PP // Y, dest % Y
    up_rows = ((dx * Y + dy) * Z + dz) * plan.E + e
    down_rows = ((dy * X + dx) * Z + dz) * plan.E + e
    up_perm = np.zeros((plan.D, plan.D))
    up_perm[up_rows, feat] = 1
    down_perm = np.zeros((plan.D, plan.D))
    down_perm[down_rows, feat] = 1
    pick = np.zeros((Z * 2 * plan.EP, plan.Q3))
    for z in range(Z):
        for half in range(2):
            for k in range(plan.E):
                pick[(z * 2 + half) * plan.EP + k, half * Z * plan.E + z * plan.E + k] = 1
    half_type = ml_dtypes.bfloat16
    return dict(
        first=first.astype(half_type),
        last=first.T.astype(half_type),
        cos=np.cos(twist).astype(np.float32),
        sin=np.sin(twist).astype(np.float32),
        inner=inner.astype(half_type),
        back=inner.T.astype(half_type),
        spread=spread.astype(half_type),
        gather=spread.T.astype(half_type),
        up_perm=up_perm.astype(half_type),
        down_perm=down_perm.astype(half_type),
        pick=pick.astype(half_type),
    )


def dot(left, right):
    return jnp.dot(left, right, preferred_element_type=F32)


def dot_t(left, right):
    return lax.dot_general(left, right, (((1,), (1,)), ((), ())), preferred_element_type=F32)


TABLE_NAMES = (S.spread, S.down_perm, S.first, S.cos, S.sin, S.inner, S.back, S.last, S.gather)
TABLE_NAMES = TABLE_NAMES + (S.up_perm, S.pick)
LOAD_NAMES = (S.spec, S.ngain, S.mgain, S.tok, S.filt, S.inw, S.cot, S.outw, S.upw, S.dnw)
SEM_NAMES = (S.tok, S.halo_a, S.halo_b, S.cot, S.gain, S.outw, S.spec1, S.spec2, S.f1a, S.f2a, S.r1a, S.r2a)
SEM_NAMES = SEM_NAMES + (S.f1b, S.f2b, S.r1b, S.r2b, S.mix, S.back, S.down, S.edge, S.inp)
SEM_NAMES = SEM_NAMES + (S.inq, S.mu, S.md, S.t3 + "a", S.t3 + "b")
for step in "1234":
    for half in "ab":
        SEM_NAMES = SEM_NAMES + tuple(name + half + step for name in (S.gu, S.gd, S.u2, S.d2))
SEMS = {name: 2 * place for place, name in enumerate(SEM_NAMES)}


def make_kernel(plan):
    n, Z, X, Y, PP, D, C, F = plan.n, plan.Z, plan.X, plan.Y, plan.P, plan.D, plan.C, plan.F
    KP, R, ZB, PB, E, EP = plan.KP, plan.R, plan.ZB, plan.PB, plan.E, plan.EP
    QX, QY = D // X, D // Y
    ROW = Z * E
    inv_d = 1.0 / D

    scratch = dict(
        spec=((2, TOK, C), F32),
        ngain=((C,), F32),
        mgain=((C,), F32),
        filt=((3, 3, C), F32),
        tokf=((HALO + TOK, D), BF16),
        inb=((HALO + TOK, D), BF16),
        cotf=((TOK, D), BF16),
        gain_src=((16, C), F32),
        gains=((16, D), F32),
        inw=((3, D, C), BF16),
        outw=((D, D), BF16),
        upw=((D, F), BF16),
        dnw=((D, F), BF16),
        s0=((Z * 2 * ZB, TOK), BF16),
        r0=((Z * 2 * ZB, TOK), BF16),
        s0b=((PP * 2 * PB, TOK), BF16),
        r0b=((PP * 2 * PB, TOK), BF16),
        spec_re=((R, TOK), F32),
        spec_im=((R, TOK), F32),
        s1=((2, C, TOK), BF16),
        r1=((2, C, TOK), BF16),
        s2=((2, R, TOK), BF16),
        r2=((2, R, TOK), BF16),
        s3=((2, R, TOK), BF16),
        r3=((2, R, TOK), BF16),
        s4=((2, C, TOK), BF16),
        r4=((2, C, TOK), BF16),
        v=((2 * R, TOK), BF16),
        wave=((2 * R, TOK), F32),
        pair=((R, 2 * TOK), BF16),
        freq=((R, 2 * TOK), F32),
        shorted=((3, TOK, C), F32),
        conv=((TOK, C), F32),
        mixf=((TOK, D), BF16),
        resid=((TOK, D), F32),
        n2=((TOK, D), F32),
        mlp=((TOK, D), BF16),
        dhid=((TOK, F), F32),
        back=((TOK, D), F32),
        back_r=((TOK, D), F32),
        down=((TOK, D), F32),
        down_r=((TOK, C), F32),
        dres=((TOK, D), F32),
        dshort=((3, TOK + 8, C), F32),
        edge=((3, 8, C), F32),
        inp=((TOK, D), F32),
        inp_r=((TOK, D), F32),
        gtok=((TOK, D), F32),
        mup=((D, TOK), BF16),
        cdn=((D, TOK), BF16),
        mu=((QX, X * TOK), BF16),
        md=((QY, Y * TOK), BF16),
        gu=((X * TOK, F), BF16),
        gd=((Y * TOK, F), BF16),
        u2s=((QX, F), BF16),
        u2p=((2, 2, ROW, F // 4), BF16),
        u2r=((2, ROW, F), BF16),
        d2s=((QY, F), BF16),
        d2p=((2, 2, ROW, F // 4), BF16),
        d2r=((2, ROW, F), BF16),
        t3i=((plan.Q3, F), BF16),
        t3s=((Z * 2 * EP, F), BF16),
        t3r=((Z, 2 * EP, F), BF16),
    )
    names = list(scratch)
    shapes = tables(plan)

    def kernel(*refs):
        it = iter(refs)
        tok, ngain_h, inw_h, filt_h, spec_h, outw_h, mgain_h, upw_h, dnw_h, cot = (
            next(it) for _ in range(10)
        )
        tab_h = Box((name, next(it)) for name in TABLE_NAMES)
        out_ref, gtok_ref, gup_ref, gdn_ref = (next(it) for _ in range(4))
        b = Box((name, next(it)) for name in names)
        tab = Box((name, next(it)) for name in TABLE_NAMES)
        sems = next(it)
        loads = next(it)

        s = lax.axis_index("seq")
        h = lax.axis_index("hid")
        z = s // PP
        p = s % PP
        x = p // Y
        y = p % Y
        other = (s, 1 - h)
        nxt = lax.rem(s + 1, n)
        prv = lax.rem(s + n - 1, n)

        barrier = pltpu.get_barrier_semaphore()

        def greet(dev):
            pl.semaphore_signal(barrier, inc=1, device_id=dev, device_id_type=MESH)

        for k in sorted(range(1, Z), key=lambda k: -min(k, Z - k)):
            greet((lax.rem(z + k, Z) * PP + p, h))
        for k in range(1, PP):
            greet((z * PP + lax.rem(p + k, PP), h))
        greet(other)
        for core in range(2):
            greet((nxt, core))
            greet((prv, core))

        landing, leaving = {}, {}

        def send(src, dst, name, dev, arrives=None, leaves=None):
            k = SEMS[name]
            landing[name] = dst if arrives is None else arrives
            leaving[name] = src if leaves is None else leaves
            pltpu.make_async_remote_copy(
                src_ref=src,
                dst_ref=dst,
                send_sem=sems.at[k],
                recv_sem=sems.at[k + 1],
                device_id=dev,
                device_id_type=MESH,
            ).start()

        def got(name):
            ref = landing.pop(name)
            pltpu.make_async_copy(ref, ref, sems.at[SEMS[name] + 1]).wait()

        def sent(name):
            ref = leaving.pop(name)
            pltpu.make_async_copy(ref, ref, sems.at[SEMS[name]]).wait()

        def cols(index, size):
            return pl.ds(pl.multiple_of(index * size, 128), size)

        def rows(index, size):
            return pl.ds(pl.multiple_of(index * size, 16), size)

        own = cols(h, C)
        filt, spec = b.filt, b.spec

        load_list = [
            (spec_h, b.spec),
            (ngain_h, b.ngain),
            (mgain_h, b.mgain),
            (tok, b.tokf.at[HALO:, own]),
            (filt_h, b.filt),
            (inw_h, b.inw),
            (cot, b.cotf.at[:, own]),
            (outw_h, b.outw.at[rows(h, C)]),
            (upw_h, b.upw),
            (dnw_h, b.dnw),
        ] + [(tab_h[name], tab[name]) for name in TABLE_NAMES]
        load_at = {name: k for k, name in enumerate(LOAD_NAMES + TABLE_NAMES)}
        load_copies = [
            pltpu.make_async_copy(src, dst, loads.at[k]) for k, (src, dst) in enumerate(load_list)
        ]
        for copy in load_copies:
            copy.start()

        def loaded(*which):
            for name in which:
                load_copies[load_at[name]].wait()

        loaded(S.ngain, S.mgain)
        g16 = jnp.concatenate(
            [jnp.broadcast_to(b[name][...][None, :], (8, C)) for name in (S.ngain, S.mgain)], axis=0
        )
        b.gain_src[...] = g16
        b.gains[:, own] = g16
        loaded(S.spec)
        for part in range(2):
            turned = jnp.transpose(spec[part]).astype(BF16)
            for k in range(Z):
                at = (2 * k + part) * ZB
                b.s0[at : at + ZB, :] = turned[k * ZB : (k + 1) * ZB, :]

        pl.semaphore_wait(barrier, Z - 1 + PP - 1 + 1 + 4)

        send(tok, b.tokf.at[HALO:, own], S.tok, other)
        tail = tok.at[TOK - HALO :, :]
        send(tail, b.tokf.at[0:HALO, own], S.halo_a, (nxt, h))
        send(tail, b.tokf.at[0:HALO, own], S.halo_b, (nxt, 1 - h))
        send(b.gain_src, b.gains.at[:, own], S.gain, other)

        z_order = sorted(range(1, Z), key=lambda k: -min(k, Z - k))
        p_order = sorted(
            range(1, PP), key=lambda k: -min(k // Y, X - k // Y) - min(k % Y, Y - k % Y)
        )

        def z_send(src, dst, size, name):
            for k in z_order:
                to = lax.rem(z + k, Z)
                some = pl.ds(0, (Z - 1) * size)
                send(
                    src.at[rows(to, size)],
                    dst.at[rows(z, size)],
                    name,
                    (to * PP + p, h),
                    dst.at[some],
                    src.at[some],
                )

        def p_send(src, dst, size, name):
            for k in p_order:
                to = lax.rem(x + k // Y, X) * Y + lax.rem(y + k % Y, Y)
                some = pl.ds(0, (PP - 1) * size)
                send(
                    src.at[rows(to, size)],
                    dst.at[rows(p, size)],
                    name,
                    (z * PP + to, h),
                    dst.at[some],
                    src.at[some],
                )

        z_send(b.s0, b.r0, 2 * ZB, S.spec1)
        b.r0[rows(z, 2 * ZB), :] = b.s0[rows(z, 2 * ZB), :]
        send(cot, b.cotf.at[:, own], S.cot, other)
        send(outw_h, b.outw.at[rows(h, C)], S.outw, other)

        got(S.tok)
        got(S.halo_a)
        got(S.halo_b)
        got(S.gain)
        loaded(S.tok, S.filt, S.inw)
        norm_gain = b.gains[0:1, :]
        mlp_gain = b.gains[8:9, :]
        tokens = b.tokf[...].astype(F32)
        scale_in = lax.rsqrt(jnp.sum(tokens * tokens, axis=1, keepdims=True) * inv_d + EPSILON)
        row = lax.broadcasted_iota(jnp.int32, (HALO + TOK, 1), 0)
        keep = jnp.logical_or(row >= HALO, s > 0)
        b.inb[...] = jnp.where(keep, tokens * scale_in * norm_gain, 0.0).astype(BF16)
        for j in range(3):
            proj = dot(b.inb[...], b.inw[j])
            total = filt[j, 0:1, :] * proj
            for i in range(1, 3):
                total = total + filt[j, i : i + 1, :] * pltpu.roll(proj, i, 0)
            b.shorted[j] = total[HALO:, :]

        def conv_out(value, a, mark):
            turned = jnp.transpose(value).astype(BF16)
            b.s1[a] = turned
            b.r1[a, rows(z, ZB), :] = b.s1[a, rows(z, ZB), :]
            z_send(b.s1.at[a], b.r1.at[a], ZB, S.f1 + mark)

        def conv_plane(a, mark):
            got(S.f1 + mark)
            b.s2[a] = dot(tab.spread[...], b.r1[a]).astype(BF16)
            b.r2[a, rows(p, PB), :] = b.s2[a, rows(p, PB), :]
            p_send(b.s2.at[a], b.r2.at[a], PB, S.f2 + mark)

        def conv_work(a, mark, sign):
            got(S.f2 + mark)
            arrived = b.r2[a]
            b.wave[...] = dot(tab.first[...], arrived)
            cosine = tab.cos[...]
            sine = tab.sin[...]
            yr = b.wave[0:R, :]
            yi = b.wave[R:, :]
            b.pair[:, 0:TOK] = (yr * cosine + yi * sine).astype(BF16)
            b.pair[:, TOK:] = (yi * cosine - yr * sine).astype(BF16)
            b.freq[...] = dot(b.pair[...], tab.inner[...])
            kr = b.spec_re[...]
            ki = sign * b.spec_im[...]
            fr = b.freq[:, 0:TOK]
            fi = b.freq[:, TOK:]
            b.pair[:, 0:TOK] = (kr * fr - ki * fi).astype(BF16)
            b.pair[:, TOK:] = (kr * fi + ki * fr).astype(BF16)
            b.freq[...] = dot(b.pair[...], tab.back[...])
            wr = b.freq[:, 0:TOK]
            wi = b.freq[:, TOK:]
            b.v[0:R, :] = (wr * cosine - wi * sine).astype(BF16)
            b.v[R:, :] = (wi * cosine + wr * sine).astype(BF16)
            b.s3[a] = (dot(tab.last[...], b.v[...]) * (1.0 / (n * TOK))).astype(BF16)
            b.r3[a, rows(p, PB), :] = b.s3[a, rows(p, PB), :]
            p_send(b.s3.at[a], b.r3.at[a], PB, S.r1 + mark)

        def conv_return(a, mark):
            got(S.r1 + mark)
            b.s4[a] = dot(tab.gather[...], b.r3[a]).astype(BF16)
            b.r4[a, rows(z, ZB), :] = b.s4[a, rows(z, ZB), :]
            z_send(b.s4.at[a], b.r4.at[a], ZB, S.r2 + mark)

        def conv_in(a, mark):
            got(S.r2 + mark)
            return jnp.transpose(b.r4[a].astype(F32))

        conv_out(b.shorted[1] * b.shorted[0], 0, "a")

        loaded(S.spread)
        got(S.spec1)
        for part in range(2):
            picked = [
                b.r0[(2 * k + part) * ZB : (2 * k + part + 1) * ZB, :] for k in range(Z)
            ]
            placed = dot(tab.spread[...], jnp.concatenate(picked, axis=0)).astype(BF16)
            for k in range(PP):
                at = (2 * k + part) * PB
                b.s0b[at : at + PB, :] = placed[k * PB : (k + 1) * PB, :]
        p_send(b.s0b, b.r0b, 2 * PB, S.spec2)
        b.r0b[rows(p, 2 * PB), :] = b.s0b[rows(p, 2 * PB), :]

        conv_plane(0, "a")

        loaded(S.dnw, S.down_perm, S.cot)
        got(S.cot)
        FH = F // 2
        wide = min(FH, 256)

        @pl.loop(0, F // wide)
        def _(k):
            at = cols(k, wide)
            b.dhid[:, at] = dot(b.cotf[...], b.dnw[:, at])

        got(S.spec2)
        for k in range(PP):
            for part, name in enumerate((S.spec_re, S.spec_im)):
                at = (2 * k + part) * PB
                b[name][k * PB : (k + 1) * PB, :] = b.r0b[at : at + PB, :].astype(F32)
        loaded(S.first, S.last, S.cos, S.sin, S.inner, S.back, S.gather)
        conv_work(0, "a", 1.0)
        loaded(S.outw, S.upw, S.up_perm, S.pick)
        got(S.outw)
        b.cdn[...] = dot_t(tab.down_perm[...], b.cotf[...]).astype(BF16)
        conv_return(0, "a")
        conv = conv_in(0, "a")
        b.conv[...] = conv
        b.mixf[:, own] = (b.shorted[2] * conv).astype(BF16)
        send(b.mixf.at[:, own], b.mixf.at[:, own], S.mix, other)
        got(S.mix)

        resid = b.tokf[HALO:, :].astype(F32) + dot(b.mixf[...], b.outw[...])
        b.resid[...] = resid
        scale_two = lax.rsqrt(jnp.sum(resid * resid, axis=1, keepdims=True) * inv_d + EPSILON)
        normed = resid * scale_two
        b.n2[...] = normed
        b.mlp[...] = (normed * mlp_gain).astype(BF16)

        def at_x(k):
            return (z * PP + k * Y + y, h)

        def at_y(k):
            return (z * PP + x * Y + k, h)

        mu_all = b.mu.at[:, pl.ds(0, (X - 1) * TOK)]
        md_all = b.md.at[:, pl.ds(0, (Y - 1) * TOK)]
        HALF = TOK // 2
        FQ = FH // 2
        halves = (pl.ds(0, FH), pl.ds(FH, FH))
        marks = ("a", "b")

        def ring_start(ref, i, size, at, name, c):
            name = name + marks[c]
            if size == 2:
                block = ref.at[rows(i, TOK), halves[c]]
                send(block, block, name + "3", at(1 - i))
                return
            right, left = lax.rem(i + 1, size), lax.rem(i + size - 1, size)
            low = ref.at[rows(2 * i, HALF), halves[c]]
            high = ref.at[rows(2 * i + 1, HALF), halves[c]]
            rest = ref.at[pl.ds(0, 2 * TOK), halves[c]]
            send(low, low, name + "1", at(right))
            send(high, high, name + "2", at(left))
            send(high, high, name + "3", at(right), rest, rest)
            send(low, low, name + "3", at(left), rest, rest)

        def ring_relay(ref, i, size, at, name, c):
            name = name + marks[c]
            if size == 2:
                return
            right, left = lax.rem(i + 1, size), lax.rem(i + size - 1, size)
            rest = ref.at[pl.ds(0, 2 * TOK), halves[c]]
            got(name + "1")
            low = ref.at[rows(2 * left, HALF), halves[c]]
            send(low, low, name + "3", at(right), rest, rest)
            got(name + "2")
            high = ref.at[rows(2 * right + 1, HALF), halves[c]]
            send(high, high, name + "3", at(left), rest, rest)

        def sum_start(src, i, size, at, name, c):
            put = b[name + S.r]
            if size == 2:
                send(
                    src.at[rows(1 - i, ROW), halves[c]],
                    put.at[0, :, halves[c]],
                    name + marks[c] + "3",
                    at(1 - i),
                )
                return
            right, left = lax.rem(i + 1, size), lax.rem(i + size - 1, size)
            far_rows = rows(lax.rem(i + 2, size), ROW)
            over = b[name + S.p]
            for side, to in ((0, right), (1, left)):
                part = pl.ds(c * FH + side * FQ, FQ)
                send(
                    src.at[far_rows, part],
                    over.at[c, side],
                    name + marks[c] + "12"[side],
                    at(to),
                )

        def sum_relay(src, i, size, at, name, c):
            if size == 2:
                return
            put, over = b[name + S.r], b[name + S.p]
            right, left = lax.rem(i + 1, size), lax.rem(i + size - 1, size)
            for side, to in ((0, right), (1, left)):
                part = pl.ds(c * FH + side * FQ, FQ)
                got(name + marks[c] + "12"[side])
                more = src[rows(to, ROW), part].astype(F32) + over[c, side].astype(F32)
                src[rows(to, ROW), part] = more.astype(BF16)
                send(
                    src.at[rows(to, ROW), halves[c]],
                    put.at[side, :, halves[c]],
                    name + marks[c] + "34"[side],
                    at(to),
                )

        def sum_end(src, i, size, name, c):
            put = b[name + S.r]
            got(name + marks[c] + "3")
            total = src[rows(i, ROW), halves[c]].astype(F32) + put[0, :, halves[c]].astype(F32)
            if size == 2:
                return total
            got(name + marks[c] + "4")
            return total + put[1, :, halves[c]].astype(F32)

        def grads_relay(c):
            ring_relay(b.gu, x, X, at_x, S.gu, c)
            ring_relay(b.gd, y, Y, at_y, S.gd, c)

        def grads_local(c):
            got(S.gu + marks[c] + "3")
            if c == 0:
                got(S.mu)

            @pl.loop(c * (FH // wide), (c + 1) * (FH // wide))
            def _(k):
                at = cols(k, wide)
                b.u2s[:, at] = dot(b.mu[...], b.gu[:, at]).astype(BF16)

            sum_start(b.u2s, y, Y, at_y, S.u2, c)
            got(S.gd + marks[c] + "3")
            if c == 0:
                got(S.md)

            @pl.loop(c * (FH // wide), (c + 1) * (FH // wide))
            def _(k):
                at = cols(k, wide)
                b.d2s[:, at] = dot(b.md[...], b.gd[:, at]).astype(BF16)

            sum_start(b.d2s, x, X, at_x, S.d2, c)

        def grads_pass(c):
            sum_relay(b.u2s, y, Y, at_y, S.u2, c)
            sum_relay(b.d2s, x, X, at_x, S.d2, c)

        def grads_z(c):
            b.t3i[0:ROW, halves[c]] = sum_end(b.u2s, y, Y, S.u2, c).astype(BF16)
            b.t3i[ROW : 2 * ROW, halves[c]] = sum_end(b.d2s, x, X, S.d2, c).astype(BF16)
            if plan.Q3 > 2 * ROW:
                b.t3i[2 * ROW :, halves[c]] = jnp.zeros((plan.Q3 - 2 * ROW, FH), BF16)
            b.t3s[:, halves[c]] = dot(tab.pick[...], b.t3i[:, halves[c]]).astype(BF16)
            t3_all = b.t3r.at[pl.ds(0, Z - 1), :, halves[c]]
            for k in z_order:
                to = lax.rem(z + k, Z)
                send(
                    b.t3s.at[rows(to, 2 * EP), halves[c]],
                    b.t3r.at[z, :, halves[c]],
                    S.t3 + marks[c],
                    (to * PP + p, h),
                    t3_all,
                    t3_all,
                )
            b.t3r[z, :, halves[c]] = b.t3s[rows(z, 2 * EP), halves[c]]

        for c in range(2):

            @pl.loop(c * (FH // wide), (c + 1) * (FH // wide))
            def _(k):
                at = cols(k, wide)
                pre = dot(b.mlp[...], b.upw[:, at])
                tanh = jnp.tanh(GELU_SCALE * (pre + 0.044715 * pre * pre * pre))
                b.gd[rows(y, TOK), at] = (0.5 * pre * (1.0 + tanh)).astype(BF16)
                slope = 0.5 * (1.0 + tanh) + 0.5 * pre * (1.0 - tanh * tanh) * GELU_SCALE * (
                    1.0 + 3.0 * 0.044715 * pre * pre
                )
                b.gu[rows(x, TOK), at] = (b.dhid[:, at] * slope).astype(BF16)

            ring_start(b.gu, x, X, at_x, S.gu, c)
            ring_start(b.gd, y, Y, at_y, S.gd, c)

        hidden = b.gd.at[rows(y, TOK)]
        d_pre = b.gu.at[rows(x, TOK)]
        for k in range(D // 256):
            at = slice(k * 256, (k + 1) * 256)
            b.back[:, at] = dot_t(d_pre[...], b.upw[at, :])
        send(b.back, b.back_r, S.back, other)
        b.mup[...] = dot_t(tab.up_perm[...], b.mlp[...]).astype(BF16)
        for k in range(1, X):
            to = lax.rem(x + k, X)
            send(
                b.mup.at[rows(to, QX)],
                b.mu.at[:, cols(x, TOK)],
                S.mu,
                at_x(to),
                mu_all,
                mu_all,
            )
        for k in range(1, Y):
            to = lax.rem(y + k, Y)
            send(
                b.cdn.at[rows(to, QY)],
                b.md.at[:, cols(y, TOK)],
                S.md,
                at_y(to),
                md_all,
                md_all,
            )
        b.mu[:, cols(x, TOK)] = b.mup[rows(x, QX), :]
        b.md[:, cols(y, TOK)] = b.cdn[rows(y, QY), :]

        got(S.back)
        d_n2 = (b.back[...] + b.back_r[...]) * mlp_gain
        normed = b.n2[...]
        inner = jnp.sum(d_n2 * normed, axis=1, keepdims=True) * inv_d
        d_resid = b.cotf[...].astype(F32) + scale_two * (d_n2 - normed * inner)
        b.dres[...] = d_resid
        d_mixed = dot_t(d_resid.astype(BF16), b.outw[rows(h, C), :])
        d_outer = d_mixed * b.conv[...]
        b.dshort[2, 0:TOK, :] = d_outer
        conv_out(d_mixed * b.shorted[2], 1, "b")

        grads_relay(0)
        conv_plane(1, "b")
        grads_relay(1)

        for k in range(D // 256):
            at = slice(k * 256, (k + 1) * 256)
            b.down[:, at] = dot_t(hidden[...], b.dnw[at, :])
        send(b.down.at[:, cols(1 - h, C)], b.down_r, S.down, other)
        got(S.down)
        out_ref[...] = (b.resid[:, own] + b.down[:, own] + b.down_r[...]).astype(BF16)
        conv_work(1, "b", -1.0)

        grads_local(0)
        conv_return(1, "b")
        grads_local(1)
        grads_pass(0)
        d_signal = conv_in(1, "b")
        b.dshort[0, 0:TOK, :] = d_signal * b.shorted[1]
        b.dshort[1, 0:TOK, :] = d_signal * b.shorted[0]
        for j in range(3):
            b.edge[j] = b.dshort[j, 0:8, :]
        send(b.edge, b.dshort.at[:, TOK:, :], S.edge, (prv, h))
        grads_z(0)
        grads_pass(1)

        MAIN = TOK - HALO
        for j in range(3):
            value = b.dshort[j, 0:TOK, :]
            total = filt[j, 0:1, :] * value
            for i in range(1, 3):
                total = total + filt[j, i : i + 1, :] * pltpu.roll(value, TOK - i, 0)
            part = dot_t(total[0:MAIN, :].astype(BF16), b.inw[j])
            if j == 0:
                b.inp[0:MAIN, :] = part
            else:
                b.inp[0:MAIN, :] += part
        send(b.inp.at[0:MAIN], b.inp_r.at[0:MAIN], S.inp, other)
        got(S.edge)
        last = s == n - 1
        row = lax.broadcasted_iota(jnp.int32, (HALO + 8, 1), 0)
        keep = jnp.logical_or(row < HALO, jnp.logical_not(last))
        for j in range(3):
            value = jnp.where(keep, b.dshort[j, MAIN:, :], 0.0)
            total = filt[j, 0:1, :] * value
            for i in range(1, 3):
                total = total + filt[j, i : i + 1, :] * pltpu.roll(value, HALO + 8 - i, 0)
            part = dot_t(total[0:HALO, :].astype(BF16), b.inw[j])
            if j == 0:
                b.inp[MAIN:, :] = part
            else:
                b.inp[MAIN:, :] += part
        send(b.inp.at[MAIN:], b.inp_r.at[MAIN:], S.inq, other)
        grads_z(1)
        got(S.inq)
        got(S.inp)
        d_n1 = (b.inp[...] + b.inp_r[...]) * norm_gain
        tokens = b.tokf[HALO:, :].astype(F32)
        scale_in = lax.rsqrt(jnp.sum(tokens * tokens, axis=1, keepdims=True) * inv_d + EPSILON)
        normed = tokens * scale_in
        inner = jnp.sum(d_n1 * normed, axis=1, keepdims=True) * inv_d
        b.gtok[...] = b.dres[...] + scale_in * (d_n1 - normed * inner)
        gtok_ref[...] = b.gtok[:, own].astype(BF16)

        got(S.t3 + "a")
        got(S.t3 + "b")
        total = b.t3r[0].astype(F32)
        for k in range(1, Z):
            total = total + b.t3r[k].astype(F32)
        total = total * (1.0 / math.sqrt(n * TOK))
        gup_ref[...] = total[0:E, :]
        gdn_ref[...] = total[EP : EP + E, :]

        for name in list(leaving):
            sent(name)

    table_scratch = [pltpu.VMEM(shapes[name].shape, shapes[name].dtype) for name in TABLE_NAMES]
    scratch_shapes = (
        [pltpu.VMEM(*scratch[name]) for name in names]
        + table_scratch
        + [
            pltpu.SemaphoreType.DMA((2 * len(SEM_NAMES),)),
            pltpu.SemaphoreType.DMA((len(LOAD_NAMES) + len(TABLE_NAMES),)),
        ]
    )
    return kernel, scratch_shapes, shapes


def solution(mesh):
    count = mesh.shape["seq"]

    def local(tokens, norm_gain, in_weight, filters, spectrum, out_weight, mlp_gain, up, down, cot):
        rows, chans = tokens.shape
        plan = Plan(count, 2 * chans, up.shape[1])
        kernel, scratch_shapes, constants = make_kernel(plan)
        here = pl.BlockSpec(memory_space=pltpu.VMEM)
        far = pl.BlockSpec(memory_space=pl.ANY)
        in_specs = [far] * (10 + len(TABLE_NAMES))
        made = pl.pallas_call(
            kernel,
            out_shape=(
                jax.ShapeDtypeStruct((rows, chans), BF16),
                jax.ShapeDtypeStruct((rows, chans), BF16),
                jax.ShapeDtypeStruct((plan.E, plan.F), F32),
                jax.ShapeDtypeStruct((plan.E, plan.F), F32),
            ),
            in_specs=in_specs,
            out_specs=(here, here, here, here),
            scratch_shapes=scratch_shapes,
            compiler_params=pltpu.CompilerParams(
                collective_id=0, has_side_effects=True, vmem_limit_bytes=58 * 1024 * 1024
            ),
        )(
            tokens,
            norm_gain,
            in_weight,
            filters,
            spectrum,
            out_weight,
            mlp_gain,
            up,
            down,
            cot,
            *[constants[name] for name in TABLE_NAMES],
        )

        def hand_over(*refs):
            for k in range(4):
                refs[k + 4][...] = refs[k][...]

        return pl.pallas_call(
            hand_over,
            out_shape=tuple(jax.ShapeDtypeStruct(part.shape, part.dtype) for part in made),
            in_specs=[here] * 4,
            out_specs=(here,) * 4,
        )(*made)

    return jax.shard_map(
        local,
        mesh=mesh,
        in_specs=(
            P("seq", "hid"),
            P("hid"),
            P(None, None, "hid"),
            P(None, None, "hid"),
            P(None, "seq", "hid"),
            P("hid", None),
            P("hid"),
            P(None, "hid"),
            P(None, "hid"),
            P("seq", "hid"),
        ),
        out_specs=(P("seq", "hid"), P("seq", "hid"), P("seq", "hid"), P("seq", "hid")),
        check_vma=False,
    )
```

```python
import math

import jax
import jax.numpy as jnp
import ml_dtypes
import numpy as np
from jax import lax
from jax.experimental import pallas as pl
from jax.experimental.pallas import tpu as pltpu
from jax.sharding import PartitionSpec as P

EPSILON = 1e-05
GELU_SCALE = 0.7978845608028654
MESH = pl.DeviceIdType.MESH
F32 = jnp.float32
BF16 = jnp.bfloat16
GRIDS = {128: (8, 4, 4), 8: (2, 2, 2), 16: (2, 4, 2)}
TOK = 128
HALO = 16


class Names:
    def __getattr__(self, key):
        return key


class Box(dict):
    __getattr__ = dict.__getitem__


S = Names()


class Plan:
    def __init__(self, count, width, units):
        self.n = count
        self.Z, self.X, self.Y = GRIDS[count]
        self.P = self.X * self.Y
        self.D = width
        self.C = width // 2
        self.F = units
        self.KC = self.C // count
        self.KP = self.KC
        while (self.Z * self.KP) % 16:
            self.KP += 1
        self.R = count * self.KP
        self.ZB = self.C // self.Z
        self.PB = self.Z * self.KP
        self.E = width // count
        self.G = 4
        self.TR = self.G * 2 * self.E


def tables(plan):
    n, Z, X, Y, PP = plan.n, plan.Z, plan.X, plan.Y, plan.P
    KC, KP, R = plan.KC, plan.KP, plan.R
    bits = n.bit_length() - 1
    rev = np.array([int(format(q, f"0{bits}b")[::-1], 2) for q in range(n)])
    rows = np.arange(R)
    slot = rows % KP
    source = (rows // KP) % Z * PP + rows // (KP * Z)
    freq = rev[source]
    same = (slot[:, None] == slot[None, :]) & (slot[:, None] < KC)
    angle = 2 * np.pi * ((freq[:, None] * source[None, :]) % n) / n
    first = np.concatenate([same * np.cos(angle), -(same * np.sin(angle))], axis=0)
    u = np.arange(TOK)
    twist = 2 * np.pi * ((freq[:, None] * u[None, :]) % (n * TOK)) / (n * TOK)
    table = 2 * np.pi * ((u[:, None] * u[None, :]) % TOK) / TOK
    inner = np.block([[np.cos(table), -np.sin(table)], [np.sin(table), np.cos(table)]])
    spread = np.zeros((R, plan.C))
    for p in range(PP):
        for z in range(Z):
            for i in range(KC):
                spread[(p * Z + z) * KP + i, z * plan.ZB + p * KC + i] = 1
    feat = np.arange(plan.D)
    e = feat % plan.E
    dest = feat // plan.E
    dz, dx, dy = dest // PP, dest % PP // Y, dest % Y
    up_rows = ((dx * Y + dy) * Z + dz) * plan.E + e
    down_rows = ((dy * X + dx) * Z + dz) * plan.E + e
    up_perm = np.zeros((plan.D, plan.D))
    up_perm[up_rows, feat] = 1
    down_perm = np.zeros((plan.D, plan.D))
    down_perm[down_rows, feat] = 1
    pick = np.zeros((Z * plan.TR, Z * plan.TR))
    for g in range(plan.G):
        for half in range(2):
            for z in range(Z):
                for k in range(plan.E):
                    to = ((z * plan.G + g) * 2 + half) * plan.E + k
                    pick[to, ((g * 2 + half) * Z + z) * plan.E + k] = 1
    half_type = ml_dtypes.bfloat16
    return dict(
        first=first.astype(half_type),
        last=first.T.astype(half_type),
        cos=np.cos(twist).astype(np.float32),
        sin=np.sin(twist).astype(np.float32),
        inner=inner.astype(half_type),
        back=inner.T.astype(half_type),
        spread=spread.astype(half_type),
        gather=spread.T.astype(half_type),
        up_perm=up_perm.astype(half_type),
        down_perm=down_perm.astype(half_type),
        pick=pick.astype(half_type),
    )


def dot(left, right):
    return jnp.dot(left, right, preferred_element_type=F32)


def dot_t(left, right):
    return lax.dot_general(left, right, (((1,), (1,)), ((), ())), preferred_element_type=F32)


TABLE_NAMES = (S.spread, S.down_perm, S.first, S.cos, S.sin, S.inner, S.back, S.last, S.gather)
TABLE_NAMES = TABLE_NAMES + (S.up_perm, S.pick)
LOAD_NAMES = (S.spec, S.ngain, S.mgain, S.tok, S.filt, S.inw, S.cot, S.outw, S.upw, S.dnw)
SEM_NAMES = (S.tok, S.halo_a, S.halo_b, S.cot, S.gain, S.outw, S.spec1, S.spec2, S.f1a, S.f2a, S.r1a, S.r2a)
SEM_NAMES = SEM_NAMES + (S.f1b, S.f2b, S.r1b, S.r2b, S.mix, S.back, S.down, S.edge, S.inp)
SEM_NAMES = SEM_NAMES + (S.inq, S.mu, S.md, S.t3 + "a", S.t3 + "b")
for step in "1234":
    for half in "ab":
        SEM_NAMES = SEM_NAMES + tuple(name + half + step for name in (S.gu, S.gd, S.u2, S.d2))
SEMS = {name: 2 * place for place, name in enumerate(SEM_NAMES)}


def make_kernel(plan):
    n, Z, X, Y, PP, D, C, F = plan.n, plan.Z, plan.X, plan.Y, plan.P, plan.D, plan.C, plan.F
    KP, R, ZB, PB, E, G, TR = plan.KP, plan.R, plan.ZB, plan.PB, plan.E, plan.G, plan.TR
    QX, QY = D // X, D // Y
    ROW = Z * E
    inv_d = 1.0 / D

    scratch = dict(
        spec=((2, TOK, C), F32),
        ngain=((C,), F32),
        mgain=((C,), F32),
        filt=((3, 3, C), F32),
        tokf=((HALO + TOK, D), BF16),
        inb=((HALO + TOK, D), BF16),
        cotf=((TOK, D), BF16),
        gain_src=((16, C), F32),
        gains=((16, D), F32),
        inw=((3, D, C), BF16),
        outw=((D, D), BF16),
        upw=((D, F), BF16),
        dnw=((D, F), BF16),
        s0=((Z * 2 * ZB, TOK), BF16),
        r0=((Z * 2 * ZB, TOK), BF16),
        s0b=((PP * 2 * PB, TOK), BF16),
        r0b=((PP * 2 * PB, TOK), BF16),
        spec_re=((R, TOK), F32),
        spec_im=((R, TOK), F32),
        s1=((2, C, TOK), BF16),
        r1=((2, C, TOK), BF16),
        s2=((2, R, TOK), BF16),
        r2=((2, R, TOK), BF16),
        s3=((2, R, TOK), BF16),
        r3=((2, R, TOK), BF16),
        s4=((2, C, TOK), BF16),
        r4=((2, C, TOK), BF16),
        v=((2 * R, TOK), BF16),
        wave=((2 * R, TOK), F32),
        pair=((R, 2 * TOK), BF16),
        freq=((R, 2 * TOK), F32),
        shorted=((3, TOK, C), F32),
        conv=((TOK, C), F32),
        mixf=((TOK, D), BF16),
        resid=((TOK, D), F32),
        n2=((TOK, D), F32),
        mlp=((TOK, D), BF16),
        dhid=((TOK, F), F32),
        back=((TOK, D), F32),
        back_r=((TOK, D), F32),
        down=((TOK, D), F32),
        down_r=((TOK, C), F32),
        dres=((TOK, D), F32),
        dshort=((3, TOK + 8, C), F32),
        edge=((3, 8, C), F32),
        inp=((TOK, D), F32),
        inp_r=((TOK, D), F32),
        gtok=((TOK, D), F32),
        mup=((D, TOK), BF16),
        cdn=((D, TOK), BF16),
        mu=((QX, X * TOK), BF16),
        md=((QY, Y * TOK), BF16),
        gu=((X * TOK, F), BF16),
        gd=((Y * TOK, F), BF16),
        u2s=((QX, F), BF16),
        u2p=((2, ROW, F // 2), BF16),
        u2r=((2, ROW, F), BF16),
        d2s=((QY, F), BF16),
        d2p=((2, ROW, F // 2), BF16),
        d2r=((2, ROW, F), BF16),
        t3i=((Z * TR, F // G), BF16),
        t3s=((Z * TR, F // G), BF16),
        t3r=((Z, TR, F // G), BF16),
    )
    names = list(scratch)
    shapes = tables(plan)

    def kernel(*refs):
        it = iter(refs)
        tok, ngain_h, inw_h, filt_h, spec_h, outw_h, mgain_h, upw_h, dnw_h, cot = (
            next(it) for _ in range(10)
        )
        tab_h = Box((name, next(it)) for name in TABLE_NAMES)
        out_ref, gtok_ref, gup_ref, gdn_ref = (next(it) for _ in range(4))
        b = Box((name, next(it)) for name in names)
        tab = Box((name, next(it)) for name in TABLE_NAMES)
        sems = next(it)
        loads = next(it)

        s = lax.axis_index("seq")
        h = lax.axis_index("hid")
        z = s // PP
        p = s % PP
        x = p // Y
        y = p % Y
        other = (s, 1 - h)
        nxt = lax.rem(s + 1, n)
        prv = lax.rem(s + n - 1, n)

        barrier = pltpu.get_barrier_semaphore()

        def greet(dev):
            pl.semaphore_signal(barrier, inc=1, device_id=dev, device_id_type=MESH)

        for k in sorted(range(1, Z), key=lambda k: -min(k, Z - k)):
            greet((lax.rem(z + k, Z) * PP + p, h))
        for k in range(1, PP):
            greet((z * PP + lax.rem(p + k, PP), h))
        greet(other)
        for core in range(2):
            greet((nxt, core))
            greet((prv, core))

        landing, leaving = {}, {}

        def send(src, dst, name, dev, arrives=None, leaves=None):
            k = SEMS[name]
            landing[name] = dst if arrives is None else arrives
            leaving[name] = src if leaves is None else leaves
            pltpu.make_async_remote_copy(
                src_ref=src,
                dst_ref=dst,
                send_sem=sems.at[k],
                recv_sem=sems.at[k + 1],
                device_id=dev,
                device_id_type=MESH,
            ).start()

        def got(name):
            ref = landing.pop(name)
            pltpu.make_async_copy(ref, ref, sems.at[SEMS[name] + 1]).wait()

        def sent(name):
            ref = leaving.pop(name)
            pltpu.make_async_copy(ref, ref, sems.at[SEMS[name]]).wait()

        def cols(index, size):
            return pl.ds(pl.multiple_of(index * size, 128), size)

        def rows(index, size):
            return pl.ds(pl.multiple_of(index * size, 16), size)

        own = cols(h, C)
        filt, spec = b.filt, b.spec

        load_list = [
            (spec_h, b.spec),
            (ngain_h, b.ngain),
            (mgain_h, b.mgain),
            (tok, b.tokf.at[HALO:, own]),
            (filt_h, b.filt),
            (inw_h, b.inw),
            (cot, b.cotf.at[:, own]),
            (outw_h, b.outw.at[rows(h, C)]),
            (upw_h, b.upw),
            (dnw_h, b.dnw),
        ] + [(tab_h[name], tab[name]) for name in TABLE_NAMES]
        load_at = {name: k for k, name in enumerate(LOAD_NAMES + TABLE_NAMES)}
        load_copies = [
            pltpu.make_async_copy(src, dst, loads.at[k]) for k, (src, dst) in enumerate(load_list)
        ]
        for copy in load_copies:
            copy.start()

        def loaded(*which):
            for name in which:
                load_copies[load_at[name]].wait()

        loaded(S.ngain, S.mgain)
        g16 = jnp.concatenate(
            [jnp.broadcast_to(b[name][...][None, :], (8, C)) for name in (S.ngain, S.mgain)], axis=0
        )
        b.gain_src[...] = g16
        b.gains[:, own] = g16
        loaded(S.spec)
        for part in range(2):
            turned = jnp.transpose(spec[part]).astype(BF16)
            for k in range(Z):
                at = (2 * k + part) * ZB
                b.s0[at : at + ZB, :] = turned[k * ZB : (k + 1) * ZB, :]

        pl.semaphore_wait(barrier, Z - 1 + PP - 1 + 1 + 4)

        send(tok, b.tokf.at[HALO:, own], S.tok, other)
        tail = tok.at[TOK - HALO :, :]
        send(tail, b.tokf.at[0:HALO, own], S.halo_a, (nxt, h))
        send(tail, b.tokf.at[0:HALO, own], S.halo_b, (nxt, 1 - h))
        send(b.gain_src, b.gains.at[:, own], S.gain, other)

        z_order = sorted(range(1, Z), key=lambda k: -min(k, Z - k))
        p_order = sorted(
            range(1, PP), key=lambda k: -min(k // Y, X - k // Y) - min(k % Y, Y - k % Y)
        )

        def z_send(src, dst, size, name):
            for k in z_order:
                to = lax.rem(z + k, Z)
                some = pl.ds(0, (Z - 1) * size)
                send(
                    src.at[rows(to, size)],
                    dst.at[rows(z, size)],
                    name,
                    (to * PP + p, h),
                    dst.at[some],
                    src.at[some],
                )

        def p_send(src, dst, size, name):
            for k in p_order:
                to = lax.rem(x + k // Y, X) * Y + lax.rem(y + k % Y, Y)
                some = pl.ds(0, (PP - 1) * size)
                send(
                    src.at[rows(to, size)],
                    dst.at[rows(p, size)],
                    name,
                    (z * PP + to, h),
                    dst.at[some],
                    src.at[some],
                )

        z_send(b.s0, b.r0, 2 * ZB, S.spec1)
        b.r0[rows(z, 2 * ZB), :] = b.s0[rows(z, 2 * ZB), :]
        send(cot, b.cotf.at[:, own], S.cot, other)
        send(outw_h, b.outw.at[rows(h, C)], S.outw, other)

        got(S.tok)
        got(S.halo_a)
        got(S.halo_b)
        got(S.gain)
        loaded(S.tok, S.filt, S.inw)
        norm_gain = b.gains[0:1, :]
        mlp_gain = b.gains[8:9, :]
        tokens = b.tokf[...].astype(F32)
        scale_in = lax.rsqrt(jnp.sum(tokens * tokens, axis=1, keepdims=True) * inv_d + EPSILON)
        row = lax.broadcasted_iota(jnp.int32, (HALO + TOK, 1), 0)
        keep = jnp.logical_or(row >= HALO, s > 0)
        b.inb[...] = jnp.where(keep, tokens * scale_in * norm_gain, 0.0).astype(BF16)
        for j in range(3):
            proj = dot(b.inb[...], b.inw[j])
            total = filt[j, 0:1, :] * proj
            for i in range(1, 3):
                total = total + filt[j, i : i + 1, :] * pltpu.roll(proj, i, 0)
            b.shorted[j] = total[HALO:, :]

        def conv_out(value, a, mark):
            turned = jnp.transpose(value).astype(BF16)
            b.s1[a] = turned
            b.r1[a, rows(z, ZB), :] = b.s1[a, rows(z, ZB), :]
            z_send(b.s1.at[a], b.r1.at[a], ZB, S.f1 + mark)

        def conv_plane(a, mark):
            got(S.f1 + mark)
            b.s2[a] = dot(tab.spread[...], b.r1[a]).astype(BF16)
            b.r2[a, rows(p, PB), :] = b.s2[a, rows(p, PB), :]
            p_send(b.s2.at[a], b.r2.at[a], PB, S.f2 + mark)

        def conv_work(a, mark, sign):
            got(S.f2 + mark)
            arrived = b.r2[a]
            b.wave[...] = dot(tab.first[...], arrived)
            cosine = tab.cos[...]
            sine = tab.sin[...]
            yr = b.wave[0:R, :]
            yi = b.wave[R:, :]
            b.pair[:, 0:TOK] = (yr * cosine + yi * sine).astype(BF16)
            b.pair[:, TOK:] = (yi * cosine - yr * sine).astype(BF16)
            b.freq[...] = dot(b.pair[...], tab.inner[...])
            kr = b.spec_re[...]
            ki = sign * b.spec_im[...]
            fr = b.freq[:, 0:TOK]
            fi = b.freq[:, TOK:]
            b.pair[:, 0:TOK] = (kr * fr - ki * fi).astype(BF16)
            b.pair[:, TOK:] = (kr * fi + ki * fr).astype(BF16)
            b.freq[...] = dot(b.pair[...], tab.back[...])
            wr = b.freq[:, 0:TOK]
            wi = b.freq[:, TOK:]
            b.v[0:R, :] = (wr * cosine - wi * sine).astype(BF16)
            b.v[R:, :] = (wi * cosine + wr * sine).astype(BF16)
            b.s3[a] = (dot(tab.last[...], b.v[...]) * (1.0 / (n * TOK))).astype(BF16)
            b.r3[a, rows(p, PB), :] = b.s3[a, rows(p, PB), :]
            p_send(b.s3.at[a], b.r3.at[a], PB, S.r1 + mark)

        def conv_return(a, mark):
            got(S.r1 + mark)
            b.s4[a] = dot(tab.gather[...], b.r3[a]).astype(BF16)
            b.r4[a, rows(z, ZB), :] = b.s4[a, rows(z, ZB), :]
            z_send(b.s4.at[a], b.r4.at[a], ZB, S.r2 + mark)

        def conv_in(a, mark):
            got(S.r2 + mark)
            return jnp.transpose(b.r4[a].astype(F32))

        conv_out(b.shorted[1] * b.shorted[0], 0, "a")

        loaded(S.spread)
        got(S.spec1)
        for part in range(2):
            picked = [
                b.r0[(2 * k + part) * ZB : (2 * k + part + 1) * ZB, :] for k in range(Z)
            ]
            placed = dot(tab.spread[...], jnp.concatenate(picked, axis=0)).astype(BF16)
            for k in range(PP):
                at = (2 * k + part) * PB
                b.s0b[at : at + PB, :] = placed[k * PB : (k + 1) * PB, :]
        p_send(b.s0b, b.r0b, 2 * PB, S.spec2)
        b.r0b[rows(p, 2 * PB), :] = b.s0b[rows(p, 2 * PB), :]

        conv_plane(0, "a")

        loaded(S.dnw, S.down_perm, S.cot)
        got(S.cot)
        FB = F // 3 if F % 384 == 0 else F // 2
        begins, sizes = (0, F - FB), (F - FB, FB)
        wide = min(FB, 256)

        @pl.loop(0, F // wide)
        def _(k):
            at = cols(k, wide)
            b.dhid[:, at] = dot(b.cotf[...], b.dnw[:, at])

        got(S.spec2)
        for k in range(PP):
            for part, name in enumerate((S.spec_re, S.spec_im)):
                at = (2 * k + part) * PB
                b[name][k * PB : (k + 1) * PB, :] = b.r0b[at : at + PB, :].astype(F32)
        loaded(S.first, S.last, S.cos, S.sin, S.inner, S.back, S.gather)
        conv_work(0, "a", 1.0)
        loaded(S.outw, S.upw, S.up_perm, S.pick)
        got(S.outw)
        def at_x(k):
            return (z * PP + k * Y + y, h)

        def at_y(k):
            return (z * PP + x * Y + k, h)

        mu_all = b.mu.at[:, pl.ds(0, (X - 1) * TOK)]
        md_all = b.md.at[:, pl.ds(0, (Y - 1) * TOK)]
        b.cdn[...] = dot_t(tab.down_perm[...], b.cotf[...]).astype(BF16)
        for k in range(1, Y):
            to = lax.rem(y + k, Y)
            send(
                b.cdn.at[rows(to, QY)],
                b.md.at[:, cols(y, TOK)],
                S.md,
                at_y(to),
                md_all,
                md_all,
            )
        b.md[:, cols(y, TOK)] = b.cdn[rows(y, QY), :]
        conv_return(0, "a")
        conv = conv_in(0, "a")
        b.conv[...] = conv
        b.mixf[:, own] = (b.shorted[2] * conv).astype(BF16)
        send(b.mixf.at[:, own], b.mixf.at[:, own], S.mix, other)
        got(S.mix)

        resid = b.tokf[HALO:, :].astype(F32) + dot(b.mixf[...], b.outw[...])
        b.resid[...] = resid
        scale_two = lax.rsqrt(jnp.sum(resid * resid, axis=1, keepdims=True) * inv_d + EPSILON)
        normed = resid * scale_two
        b.n2[...] = normed
        b.mlp[...] = (normed * mlp_gain).astype(BF16)

        HALF = TOK // 2
        halves = tuple(pl.ds(begin, size) for begin, size in zip(begins, sizes))
        thin = tuple(pl.ds(begin // G, size // G) for begin, size in zip(begins, sizes))
        marks = ("a", "b")

        def ring_start(ref, i, size, at, name, c):
            name = name + marks[c]
            if size == 2:
                block = ref.at[rows(i, TOK), halves[c]]
                send(block, block, name + "3", at(1 - i))
                return
            right, left = lax.rem(i + 1, size), lax.rem(i + size - 1, size)
            low = ref.at[rows(2 * i, HALF), halves[c]]
            high = ref.at[rows(2 * i + 1, HALF), halves[c]]
            send(low, low, name + "1", at(right))
            send(high, high, name + "2", at(left))

        def ring_rest(ref, i, size, at, name, c):
            name = name + marks[c]
            if size == 2:
                return
            right, left = lax.rem(i + 1, size), lax.rem(i + size - 1, size)
            low = ref.at[rows(2 * i, HALF), halves[c]]
            high = ref.at[rows(2 * i + 1, HALF), halves[c]]
            rest = ref.at[pl.ds(0, 2 * TOK), halves[c]]
            send(high, high, name + "3", at(right), rest, rest)
            send(low, low, name + "3", at(left), rest, rest)

        def ring_relay(ref, i, size, at, name, c):
            name = name + marks[c]
            if size == 2:
                return
            right, left = lax.rem(i + 1, size), lax.rem(i + size - 1, size)
            rest = ref.at[pl.ds(0, 2 * TOK), halves[c]]
            got(name + "1")
            low = ref.at[rows(2 * left, HALF), halves[c]]
            send(low, low, name + "3", at(right), rest, rest)
            got(name + "2")
            high = ref.at[rows(2 * right + 1, HALF), halves[c]]
            send(high, high, name + "3", at(left), rest, rest)

        def sum_start(src, i, size, at, name, c):
            put = b[name + S.r]
            if size == 2:
                send(
                    src.at[rows(1 - i, ROW), halves[c]],
                    put.at[0, :, halves[c]],
                    name + marks[c] + "3",
                    at(1 - i),
                )
                return
            right, left = lax.rem(i + 1, size), lax.rem(i + size - 1, size)
            far_rows = rows(lax.rem(i + 2, size), ROW)
            over = b[name + S.p]
            for side, to in ((0, right), (1, left)):
                part = pl.ds(begins[c] + side * (sizes[c] // 2), sizes[c] // 2)
                send(
                    src.at[far_rows, part],
                    over.at[side, :, pl.ds(begins[c] // 2, sizes[c] // 2)],
                    name + marks[c] + "12"[side],
                    at(to),
                )

        def sum_relay(src, i, size, at, name, c):
            if size == 2:
                return
            put, over = b[name + S.r], b[name + S.p]
            right, left = lax.rem(i + 1, size), lax.rem(i + size - 1, size)
            for side, to in ((0, right), (1, left)):
                part = pl.ds(begins[c] + side * (sizes[c] // 2), sizes[c] // 2)
                got(name + marks[c] + "12"[side])
                came = over[side, :, pl.ds(begins[c] // 2, sizes[c] // 2)]
                more = src[rows(to, ROW), part].astype(F32) + came.astype(F32)
                src[rows(to, ROW), part] = more.astype(BF16)
                send(
                    src.at[rows(to, ROW), halves[c]],
                    put.at[side, :, halves[c]],
                    name + marks[c] + "34"[side],
                    at(to),
                )

        def sum_end(src, i, size, name, c):
            put = b[name + S.r]
            got(name + marks[c] + "3")
            total = src[rows(i, ROW), halves[c]].astype(F32) + put[0, :, halves[c]].astype(F32)
            if size == 2:
                return total
            got(name + marks[c] + "4")
            return total + put[1, :, halves[c]].astype(F32)

        def grads_relay(c):
            ring_relay(b.gu, x, X, at_x, S.gu, c)
            ring_relay(b.gd, y, Y, at_y, S.gd, c)

        def grads_local(c):
            got(S.gu + marks[c] + "3")
            if c == 0:
                got(S.mu)

            @pl.loop(begins[c] // wide, (begins[c] + sizes[c]) // wide)
            def _(k):
                at = cols(k, wide)
                b.u2s[:, at] = dot(b.mu[...], b.gu[:, at]).astype(BF16)

            sum_start(b.u2s, y, Y, at_y, S.u2, c)
            got(S.gd + marks[c] + "3")
            if c == 0:
                got(S.md)

            @pl.loop(begins[c] // wide, (begins[c] + sizes[c]) // wide)
            def _(k):
                at = cols(k, wide)
                b.d2s[:, at] = dot(b.md[...], b.gd[:, at]).astype(BF16)

            sum_start(b.d2s, x, X, at_x, S.d2, c)

        def grads_pass(c):
            sum_relay(b.u2s, y, Y, at_y, S.u2, c)
            sum_relay(b.d2s, x, X, at_x, S.d2, c)

        def grads_z(c):
            width = sizes[c] // G
            for half, total in enumerate(
                (sum_end(b.u2s, y, Y, S.u2, c), sum_end(b.d2s, x, X, S.d2, c))
            ):
                for g in range(G):
                    at = (g * 2 + half) * ROW
                    b.t3i[at : at + ROW, thin[c]] = total[:, g * width : (g + 1) * width].astype(BF16)
            b.t3s[:, thin[c]] = dot(tab.pick[...], b.t3i[:, thin[c]]).astype(BF16)
            t3_all = b.t3r.at[pl.ds(0, Z - 1), :, thin[c]]
            for k in z_order:
                to = lax.rem(z + k, Z)
                send(
                    b.t3s.at[rows(to, TR), thin[c]],
                    b.t3r.at[z, :, thin[c]],
                    S.t3 + marks[c],
                    (to * PP + p, h),
                    t3_all,
                    t3_all,
                )
            b.t3r[z, :, thin[c]] = b.t3s[rows(z, TR), thin[c]]

        def grads_out(c):
            width = sizes[c] // G
            got(S.t3 + marks[c])
            total = b.t3r[0, :, thin[c]].astype(F32)
            for k in range(1, Z):
                total = total + b.t3r[k, :, thin[c]].astype(F32)
            total = total * (1.0 / math.sqrt(n * TOK))
            for g in range(G):
                at = pl.ds(begins[c] + g * width, width)
                gup_ref[:, at] = total[2 * g * E : (2 * g + 1) * E, :]
                gdn_ref[:, at] = total[(2 * g + 1) * E : (2 * g + 2) * E, :]

        for c in range(2):

            @pl.loop(begins[c] // wide, (begins[c] + sizes[c]) // wide)
            def _(k):
                at = cols(k, wide)
                pre = dot(b.mlp[...], b.upw[:, at])
                tanh = jnp.tanh(GELU_SCALE * (pre + 0.044715 * pre * pre * pre))
                b.gd[rows(y, TOK), at] = (0.5 * pre * (1.0 + tanh)).astype(BF16)
                slope = 0.5 * (1.0 + tanh) + 0.5 * pre * (1.0 - tanh * tanh) * GELU_SCALE * (
                    1.0 + 3.0 * 0.044715 * pre * pre
                )
                b.gu[rows(x, TOK), at] = (b.dhid[:, at] * slope).astype(BF16)

            ring_start(b.gu, x, X, at_x, S.gu, c)
            ring_start(b.gd, y, Y, at_y, S.gd, c)

        def grads_rest(c):
            ring_rest(b.gu, x, X, at_x, S.gu, c)
            ring_rest(b.gd, y, Y, at_y, S.gd, c)

        grads_rest(0)
        hidden = b.gd.at[rows(y, TOK)]
        d_pre = b.gu.at[rows(x, TOK)]
        for k in range(D // 256):
            at = slice(k * 256, (k + 1) * 256)
            b.back[:, at] = dot_t(d_pre[...], b.upw[at, :])
        send(b.back, b.back_r, S.back, other)
        b.mup[...] = dot_t(tab.up_perm[...], b.mlp[...]).astype(BF16)
        for k in range(1, X):
            to = lax.rem(x + k, X)
            send(
                b.mup.at[rows(to, QX)],
                b.mu.at[:, cols(x, TOK)],
                S.mu,
                at_x(to),
                mu_all,
                mu_all,
            )
        b.mu[:, cols(x, TOK)] = b.mup[rows(x, QX), :]

        got(S.back)
        d_n2 = (b.back[...] + b.back_r[...]) * mlp_gain
        normed = b.n2[...]
        inner = jnp.sum(d_n2 * normed, axis=1, keepdims=True) * inv_d
        d_resid = b.cotf[...].astype(F32) + scale_two * (d_n2 - normed * inner)
        b.dres[...] = d_resid
        d_mixed = dot_t(d_resid.astype(BF16), b.outw[rows(h, C), :])
        d_outer = d_mixed * b.conv[...]
        b.dshort[2, 0:TOK, :] = d_outer
        conv_out(d_mixed * b.shorted[2], 1, "b")

        grads_relay(0)
        conv_plane(1, "b")
        grads_rest(1)
        grads_relay(1)
        grads_local(0)

        conv_work(1, "b", -1.0)

        grads_local(1)
        grads_pass(0)
        conv_return(1, "b")
        grads_pass(1)
        grads_z(0)
        for k in range(D // 256):
            at = slice(k * 256, (k + 1) * 256)
            b.down[:, at] = dot_t(hidden[...], b.dnw[at, :])
        send(b.down.at[:, cols(1 - h, C)], b.down_r, S.down, other)
        grads_z(1)
        d_signal = conv_in(1, "b")
        b.dshort[0, 0:TOK, :] = d_signal * b.shorted[1]
        b.dshort[1, 0:TOK, :] = d_signal * b.shorted[0]
        for j in range(3):
            b.edge[j] = b.dshort[j, 0:8, :]
        send(b.edge, b.dshort.at[:, TOK:, :], S.edge, (prv, h))
        MAIN = TOK - HALO
        for j in range(3):
            value = b.dshort[j, 0:TOK, :]
            total = filt[j, 0:1, :] * value
            for i in range(1, 3):
                total = total + filt[j, i : i + 1, :] * pltpu.roll(value, TOK - i, 0)
            part = dot_t(total[0:MAIN, :].astype(BF16), b.inw[j])
            if j == 0:
                b.inp[0:MAIN, :] = part
            else:
                b.inp[0:MAIN, :] += part
        send(b.inp.at[0:MAIN], b.inp_r.at[0:MAIN], S.inp, other)
        got(S.down)
        out_ref[...] = (b.resid[:, own] + b.down[:, own] + b.down_r[...]).astype(BF16)
        got(S.edge)
        last = s == n - 1
        row = lax.broadcasted_iota(jnp.int32, (HALO + 8, 1), 0)
        keep = jnp.logical_or(row < HALO, jnp.logical_not(last))
        for j in range(3):
            value = jnp.where(keep, b.dshort[j, MAIN:, :], 0.0)
            total = filt[j, 0:1, :] * value
            for i in range(1, 3):
                total = total + filt[j, i : i + 1, :] * pltpu.roll(value, HALO + 8 - i, 0)
            part = dot_t(total[0:HALO, :].astype(BF16), b.inw[j])
            if j == 0:
                b.inp[MAIN:, :] = part
            else:
                b.inp[MAIN:, :] += part
        send(b.inp.at[MAIN:], b.inp_r.at[MAIN:], S.inq, other)
        got(S.inq)
        got(S.inp)
        d_n1 = (b.inp[...] + b.inp_r[...]) * norm_gain
        tokens = b.tokf[HALO:, :].astype(F32)
        scale_in = lax.rsqrt(jnp.sum(tokens * tokens, axis=1, keepdims=True) * inv_d + EPSILON)
        normed = tokens * scale_in
        inner = jnp.sum(d_n1 * normed, axis=1, keepdims=True) * inv_d
        b.gtok[...] = b.dres[...] + scale_in * (d_n1 - normed * inner)
        gtok_ref[...] = b.gtok[:, own].astype(BF16)

        grads_out(0)
        grads_out(1)

        for name in list(leaving):
            sent(name)

    table_scratch = [pltpu.VMEM(shapes[name].shape, shapes[name].dtype) for name in TABLE_NAMES]
    scratch_shapes = (
        [pltpu.VMEM(*scratch[name]) for name in names]
        + table_scratch
        + [
            pltpu.SemaphoreType.DMA((2 * len(SEM_NAMES),)),
            pltpu.SemaphoreType.DMA((len(LOAD_NAMES) + len(TABLE_NAMES),)),
        ]
    )
    return kernel, scratch_shapes, shapes


def solution(mesh):
    count = mesh.shape["seq"]

    def local(tokens, norm_gain, in_weight, filters, spectrum, out_weight, mlp_gain, up, down, cot):
        rows, chans = tokens.shape
        plan = Plan(count, 2 * chans, up.shape[1])
        kernel, scratch_shapes, constants = make_kernel(plan)
        here = pl.BlockSpec(memory_space=pltpu.VMEM)
        far = pl.BlockSpec(memory_space=pl.ANY)
        in_specs = [far] * (10 + len(TABLE_NAMES))
        made = pl.pallas_call(
            kernel,
            out_shape=(
                jax.ShapeDtypeStruct((rows, chans), BF16),
                jax.ShapeDtypeStruct((rows, chans), BF16),
                jax.ShapeDtypeStruct((plan.E, plan.F), F32),
                jax.ShapeDtypeStruct((plan.E, plan.F), F32),
            ),
            in_specs=in_specs,
            out_specs=(here, here, here, here),
            scratch_shapes=scratch_shapes,
            compiler_params=pltpu.CompilerParams(
                collective_id=0, has_side_effects=True, vmem_limit_bytes=58 * 1024 * 1024
            ),
        )(
            tokens,
            norm_gain,
            in_weight,
            filters,
            spectrum,
            out_weight,
            mlp_gain,
            up,
            down,
            cot,
            *[constants[name] for name in TABLE_NAMES],
        )

        def hand_over(*refs):
            for k in range(4):
                refs[k + 4][...] = refs[k][...]

        return pl.pallas_call(
            hand_over,
            out_shape=tuple(jax.ShapeDtypeStruct(part.shape, part.dtype) for part in made),
            in_specs=[here] * 4,
            out_specs=(here,) * 4,
        )(*made)

    return jax.shard_map(
        local,
        mesh=mesh,
        in_specs=(
            P("seq", "hid"),
            P("hid"),
            P(None, None, "hid"),
            P(None, None, "hid"),
            P(None, "seq", "hid"),
            P("hid", None),
            P("hid"),
            P(None, "hid"),
            P(None, "hid"),
            P("seq", "hid"),
        ),
        out_specs=(P("seq", "hid"), P("seq", "hid"), P("seq", "hid"), P("seq", "hid")),
        check_vma=False,
    )
```
